32 devices in a mesh: clip: 4 (over y, x), tm: 8 (over z, core).
Axes of the slice: x: 2, y: 2, z: 4, core: 2. Of those that a mesh axis runs over, the one named last changes fastest.
Arguments:
- x_inner: bfloat16 [32, 192, 2048], P(('clip', 'tm')), parts along dimension 0, may hold values from -6 to 6
- bc_inputs: bfloat16 [32, 192, 256], P(('clip', 'tm')), parts along dimension 0, may hold values from -2 to 2
- step_raw: bfloat16 [32, 192, 64], P(('clip', 'tm')), parts along dimension 0, may hold values from -5 to 5
- decay_rate: float32 [2, 32], replicated, may hold values from 0.002 to 0.3
- skip_gain: float32 [32], replicated, may hold values from 0.1 to 1.9
- w_out: bfloat16 [2048, 1024], P('tm'), may hold values from -0.125 to 0.125
- grad_out: bfloat16 [32, 192, 1024], P(('clip', 'tm')), parts along dimension 0, may hold values from -6 to 6
Outputs:
- mixed_out: bfloat16 [32, 192, 1024], P(('clip', 'tm')), parts along dimension 0
- grad_inner: bfloat16 [32, 192, 2048], P(('clip', 'tm')), parts along dimension 0
- grad_bc: bfloat16 [32, 192, 256], P(('clip', 'tm')), parts along dimension 0
- grad_step: bfloat16 [32, 192, 64], P(('clip', 'tm')), parts along dimension 0
- grad_w_out: float32 [8192, 1024], P(('clip', 'tm')), parts along dimension 0
The draws below stay inside these ranges and needn't reach their ends.
There are 4 independent parts, one for each index of `clip`. The reference program is written for one: setup_inputs(seed, part) draws one part's arguments, and reference() takes and returns one part's arrays. A program takes and returns all parts, laid end to end along the dimension named above; an argument that names none is the same for every part. Nothing has to cross between parts.
All inputs are finite; a program needn't handle non-finite values.
Results may differ from the reference program's by a relative error of at most 0.022.
Values may be sent and summed in bfloat16 or wider, within the bound.
A program may use at most 128 MiB of HBM per device.

```python
import math
import jax
import jax.numpy as jnp
from jax import lax

D = 1024
H = 32
N = 64
P_SIZE = 192
E = 2048
FRAMES = 8


def levels(stream_key, dims, cuts, smallest, top_value):
    def one(position, shards_of):
        steps = jax.random.uniform(jax.random.fold_in(jax.random.fold_in(stream_key, 6), position), (shards_of,), jnp.float32, smallest / len(cuts), top_value / len(cuts))
        return jnp.repeat(jnp.exp(steps), dims[position] // shards_of).reshape((-1,) + (1,) * (len(dims) - position - 1))

    factor_of = one(*cuts[0])
    for cut in cuts[1:]:
        factor_of = factor_of * one(*cut)
    return factor_of


def gaussian(rng, extent, width, most, split=(), kind=jnp.bfloat16):
    entries = width * jax.random.normal(rng, extent, jnp.float32)
    if split:
        entries = entries * levels(rng, extent, split, -0.22, 0.18)
    return jnp.clip(entries, -most, most).astype(kind)


def setup_inputs(seed: int = 0, part: int = 0) -> dict:
    seeds = jax.random.split(jax.random.key(seed), 8)
    own_keys = jax.random.split(jax.random.fold_in(seeds[7], part), 8)
    x_inner = gaussian(own_keys[0], (FRAMES, P_SIZE, E), 1.0, 6.0, ((0, 8),))
    bc_inputs = gaussian(own_keys[1], (FRAMES, P_SIZE, 4 * N), 0.25, 2.0, ((0, 8),))
    step_raw = gaussian(own_keys[2], (FRAMES, P_SIZE, 2 * H), 1.0, 5.0, ((0, 8),))
    decay_rate = jnp.clip(jnp.exp(jax.random.uniform(seeds[3], (2, H), jnp.float32, math.log(0.002), math.log(0.3))), 0.002, 0.3)
    skip_gain = jnp.clip(1.0 + 0.18 * jax.random.normal(seeds[4], (H,), jnp.float32), 0.1, 1.9)
    w_out = gaussian(seeds[5], (E, D), E ** -0.5, 0.125, ((0, 8),))
    grad_out = gaussian(own_keys[6], (FRAMES, P_SIZE, D), 1.0, 6.0, ((0, 8),))
    return dict(x_inner=x_inner, bc_inputs=bc_inputs, step_raw=step_raw, decay_rate=decay_rate, skip_gain=skip_gain, w_out=w_out, grad_out=grad_out)


HIGH = lax.Precision.HIGHEST

def block_scan(heads_in, b_rows, c_rows, step_size, decay_rates, block_len):
    length, nheads, head_dim = heads_in.shape
    block_count = length // block_len
    state_size = b_rows.shape[-1]
    x_blocks = heads_in.reshape(block_count, block_len, nheads, head_dim)
    b_blocks = b_rows.reshape(block_count, block_len, state_size)
    c_blocks = c_rows.reshape(block_count, block_len, state_size)
    s_blocks = step_size.reshape(block_count, block_len, nheads)
    log_cum = jnp.cumsum(-s_blocks * decay_rates, axis=1)
    log_gaps = log_cum[:, :, None, :] - log_cum[:, None, :, :]
    lower_mask = jnp.arange(block_len)[:, None] >= jnp.arange(block_len)[None, :]
    decay_mat = jnp.exp(jnp.where(lower_mask[None, :, :, None], log_gaps, -jnp.inf))
    gram_mat = jnp.einsum('kin,kjn->kij', c_blocks, b_blocks, precision=HIGH)
    weights = gram_mat[:, :, :, None] * decay_mat * s_blocks[:, None, :, :]
    inside = jnp.einsum('kijh,kjhd->kihd', weights, x_blocks, precision=HIGH)
    log_last = log_cum[:, -1, :]
    tail_weight = jnp.exp(log_last[:, None, :] - log_cum) * s_blocks
    states = jnp.einsum('kjh,kjhd,kjn->khdn', tail_weight, x_blocks, b_blocks, precision=HIGH)

    def advance(state_carry, inputs):
        log_end, added_state = inputs
        return (jnp.exp(log_end)[:, None, None] * state_carry + added_state, state_carry)
    final_state, entering = lax.scan(advance, jnp.zeros(states.shape[1:], states.dtype), (log_last, states))
    outside = jnp.einsum('kin,khdn->kihd', c_blocks, entering, precision=HIGH) * jnp.exp(log_cum)[:, :, :, None]
    return (inside + outside).reshape(length, nheads, head_dim)

def whole_scan(heads_in, b_rows, c_rows, step_size, decay_rates):
    length = heads_in.shape[0]
    log_cum = jnp.cumsum(-step_size * decay_rates, axis=0)
    log_gaps = log_cum[:, None, :] - log_cum[None, :, :]
    lower_mask = jnp.arange(length)[:, None] >= jnp.arange(length)[None, :]
    decay_mat = jnp.exp(jnp.where(lower_mask[:, :, None], log_gaps, -jnp.inf))
    gram_mat = jnp.einsum('in,jn->ij', c_rows, b_rows, precision=HIGH)
    weights = gram_mat[:, :, None] * decay_mat * step_size[None, :, :]
    return jnp.einsum('ijh,jhd->ihd', weights, heads_in, precision=HIGH)

def spatial_mix(x_vals, b_vals, c_vals, raw_vals, decay_rates):
    frames, patches, inner_width = x_vals.shape
    nheads = decay_rates.shape[0]
    step_size = jax.nn.softplus(raw_vals)
    heads_in = x_vals.reshape(frames, patches, nheads, inner_width // nheads)
    block_len = math.gcd(patches, 64)

    def one_frame(x_one, b_one, c_one, s_one):
        return block_scan(x_one, b_one, c_one, s_one, decay_rates, block_len)
    result = jax.vmap(one_frame)(heads_in, b_vals, c_vals, step_size)
    return result.reshape(frames, patches, inner_width)

def temporal_mix(x_vals, b_vals, c_vals, raw_vals, decay_rates, skip_gain):
    frames, patches, inner_width = x_vals.shape
    nheads = decay_rates.shape[0]
    step_size = jax.nn.softplus(raw_vals)
    heads_in = x_vals.reshape(frames, patches, nheads, inner_width // nheads)

    def one_patch(x_one, b_one, c_one, s_one):
        return whole_scan(x_one, b_one, c_one, s_one, decay_rates)
    result = jax.vmap(one_patch, in_axes=1, out_axes=1)(heads_in, b_vals, c_vals, step_size)
    result = result + skip_gain[None, None, :, None] * heads_in
    return result.reshape(frames, patches, inner_width)

def reference(x_inner, bc_inputs, step_raw, decay_rate, skip_gain, w_out, grad_out):
    state_size = bc_inputs.shape[-1] // 4
    nheads = skip_gain.shape[0]
    frames, patches, inner_width = x_inner.shape
    model_width = w_out.shape[1]

    def spatial_fn(x_vals, b_vals, c_vals, raw_vals):
        return spatial_mix(x_vals, b_vals, c_vals, raw_vals, decay_rate[0])

    def temporal_fn(x_vals, b_vals, c_vals, raw_vals):
        return temporal_mix(x_vals, b_vals, c_vals, raw_vals, decay_rate[1], skip_gain)
    spatial_out, spatial_back = jax.vjp(spatial_fn, x_inner.astype(jnp.float32), bc_inputs[:, :, :state_size].astype(jnp.float32), bc_inputs[:, :, state_size:2 * state_size].astype(jnp.float32), step_raw[:, :, :nheads].astype(jnp.float32))
    spatial_bf = lax.optimization_barrier(spatial_out.astype(jnp.bfloat16))
    mixed, temporal_back = jax.vjp(temporal_fn, spatial_bf.astype(jnp.float32), bc_inputs[:, :, 2 * state_size:3 * state_size].astype(jnp.float32), bc_inputs[:, :, 3 * state_size:].astype(jnp.float32), step_raw[:, :, nheads:].astype(jnp.float32))
    mixed_rows = mixed.astype(jnp.bfloat16).reshape(-1, inner_width)
    grad_rows = grad_out.reshape(-1, model_width)
    mixed_out = jnp.dot(mixed_rows, w_out, preferred_element_type=jnp.float32).astype(jnp.bfloat16)
    grad_mixed = lax.dot_general(grad_rows, w_out, (((1,), (1,)), ((), ())), preferred_element_type=jnp.float32)
    grad_mixed = lax.optimization_barrier(grad_mixed.astype(jnp.bfloat16))
    grad_w_out = lax.dot_general(mixed_rows, grad_rows, (((0,), (0,)), ((), ())), preferred_element_type=jnp.float32)
    grad_spatial32, grad_bt, grad_ct, grad_raw_t = temporal_back(grad_mixed.astype(jnp.float32).reshape(frames, patches, inner_width))
    grad_spatial = lax.optimization_barrier(grad_spatial32.astype(jnp.bfloat16))
    grad_x32, grad_bs, grad_cs, grad_raw_s = spatial_back(grad_spatial.astype(jnp.float32))
    grad_bc = jnp.concatenate([grad_bs, grad_cs, grad_bt, grad_ct], axis=-1).astype(jnp.bfloat16)
    grad_step = jnp.concatenate([grad_raw_s, grad_raw_t], axis=-1).astype(jnp.bfloat16)
    return (mixed_out.reshape(frames, patches, model_width), grad_x32.astype(jnp.bfloat16), grad_bc, grad_step, grad_w_out)
```

```python
import functools

import jax
import jax.numpy as jnp
from jax import lax
from jax.experimental import pallas as pl
from jax.experimental.pallas import tpu as pltpu
from jax.sharding import PartitionSpec as P

F32 = jnp.float32
BF16 = jnp.bfloat16
HIGH = lax.Precision.HIGHEST
LANES = 128


def iota(shape, dim):
    return lax.broadcasted_iota(jnp.int32, shape, dim)


def mm(a, b, ca=1, cb=0, precision=None):
    return lax.dot_general(
        a, b, (((ca,), (cb,)), ((), ())), precision=precision, preferred_element_type=F32
    )


def softplus(raw):
    return jnp.maximum(raw, 0.0) + jnp.log(1.0 + jnp.exp(-jnp.abs(raw)))


def picker(rows, base, count):
    r, c = iota((rows, LANES), 0), iota((rows, LANES), 1)
    return jnp.where((r == c + base) & (c < count), 1.0, 0.0).astype(BF16)


def steps_of(raw_bf, pick, decay_row, mask):
    raw = mm(raw_bf, pick)
    step = softplus(raw)
    cum = mm(mask, -step * decay_row, precision=HIGH)
    return raw, step, cum, step.T, cum.T


def weights_of(head, cum, cum_t, step_t):
    gap = cum[:, head : head + 1] - cum_t[head : head + 1, :]
    return jnp.exp(jnp.minimum(gap, 0.0)) * step_t[head : head + 1, :]


def step_grad(row_sums, col_sums_t, raw, step, decay_row, mask):
    col_sums = col_sums_t.T
    later = mm(mask, row_sums - col_sums, 0, 0, precision=HIGH)
    grad = col_sums / step - decay_row * later
    return grad / (1.0 + jnp.exp(-raw))


def forward_kernel(nheads, chunk, x_ref, bc_ref, raw_ref, decay_ref, out_ref):
    length = x_ref.shape[0]
    n = bc_ref.shape[1] // 4
    mask = jnp.where(iota((length, length), 0) >= iota((length, length), 1), 1.0, 0.0)
    pick = picker(raw_ref.shape[1], 0, nheads)
    _, _, cum, step_t, cum_t = steps_of(raw_ref[...], pick, decay_ref[0:1, :], mask)
    gram = mm(bc_ref[:, n : 2 * n], bc_ref[:, :n], 1, 1) * mask
    first = iota((length, LANES), 1) < LANES // 2
    for pair in range(nheads // 2):
        xp = x_ref[:, pair * LANES : (pair + 1) * LANES]
        ys = []
        for e in range(2):
            m = gram * weights_of(2 * pair + e, cum, cum_t, step_t)
            ys.append(mm(m.astype(BF16), xp))
        at = pair * LANES
        out_ref[at // chunk, :, at % chunk : at % chunk + LANES] = jnp.where(
            first, ys[0], ys[1]
        ).astype(BF16)


def backward_kernel(
    nheads, chunk, x_ref, bc_ref, raw_ref, decay_ref, dy_ref, dx_ref, dbc_ref, draw_ref
):
    length = x_ref.shape[0]
    n = bc_ref.shape[1] // 4
    mask = jnp.where(iota((length, length), 0) >= iota((length, length), 1), 1.0, 0.0)
    pick = picker(raw_ref.shape[1], 0, nheads)
    decay_row = decay_ref[0:1, :]
    raw, step, cum, step_t, cum_t = steps_of(raw_ref[...], pick, decay_row, mask)
    b, c = bc_ref[:, :n], bc_ref[:, n : 2 * n]
    gram = mm(c, b, 1, 1) * mask
    lane = iota((length, LANES), 1)
    first = lane < LANES // 2
    sub = iota((LANES, length), 0)
    dgram = jnp.zeros((length, length), F32)
    row_sums = jnp.zeros((length, LANES), F32)
    col_sums = jnp.zeros((LANES, length), F32)
    for pair in range(nheads // 2):
        at = pair * LANES
        xp = x_ref[:, at : at + LANES]
        gp = dy_ref[at // chunk, :, at % chunk : at % chunk + LANES]
        dxs = []
        for e in range(2):
            head = 2 * pair + e
            ls = weights_of(head, cum, cum_t, step_t)
            m = gram * ls
            ge = jnp.where(first if e == 0 else ~first, gp, jnp.zeros_like(gp))
            dm = mm(ge, xp, 1, 1)
            dgram = dgram + dm * ls
            w = dm * m
            row_sums = jnp.where(lane == head, jnp.sum(w, axis=1, keepdims=True), row_sums)
            col_sums = jnp.where(sub == head, jnp.sum(w, axis=0, keepdims=True), col_sums)
            dxs.append(mm(m.astype(BF16), gp, 0, 0))
        dx_ref[:, at : at + LANES] = jnp.where(first, dxs[0], dxs[1]).astype(BF16)
    draw = step_grad(row_sums, col_sums, raw, step, decay_row, mask)
    draw_ref[...] = draw[:, :nheads].astype(BF16)
    dgb = (dgram * mask).astype(BF16)
    dbc_ref[:, :n] = mm(dgb, c, 0, 0).astype(BF16)
    dbc_ref[:, n:] = mm(dgb, b).astype(BF16)


def temporal_kernel(
    nheads, mine, group,
    base_ref, decay_ref, skip_ref, x_ref, go_ref, aux_ref, w_ref,
    dx_ref, part_ref, daux_ref, gw_ref, mixed_ref,
):
    frames, patches, width = x_ref.shape
    n = (aux_ref.shape[2] - nheads) // 2
    base = base_ref[0]
    rows = frames * group
    ri, ci = iota((rows, rows), 0), iota((rows, rows), 1)
    mask = jnp.where((ri % group == ci % group) & (ri >= ci), 1.0, 0.0)
    pick = picker(nheads, base, mine)
    lane = iota((rows, LANES), 1)
    sub = iota((LANES, rows), 0)
    first = lane < LANES // 2
    lane1 = iota((1, LANES), 1)
    decay_row = jnp.zeros((1, LANES), F32)
    for h in range(mine):
        decay_row = jnp.where(lane1 == h, decay_ref[1, base + h], decay_row)
    w = w_ref[...]
    go = go_ref[...].reshape(frames * patches, go_ref.shape[2])
    carried = mm(go, w, 1, 1).astype(BF16).reshape(frames, patches, width)
    for part in range(patches // group):
        sl = slice(part * group, (part + 1) * group)
        x = x_ref[:, sl, :].reshape(rows, width)
        g = carried[:, sl, :].reshape(rows, width)
        aux = aux_ref[:, sl, :].reshape(rows, aux_ref.shape[2])
        b, c = aux[:, :n], aux[:, n : 2 * n]
        raw, step, cum, step_t, cum_t = steps_of(aux[:, 2 * n :], pick, decay_row, mask)
        gram = mm(c, b, 1, 1) * mask
        dgram = jnp.zeros((rows, rows), F32)
        row_sums = jnp.zeros((rows, LANES), F32)
        col_sums = jnp.zeros((LANES, rows), F32)
        for pair in range(mine // 2):
            at = pair * LANES
            xp, gp = x[:, at : at + LANES], g[:, at : at + LANES]
            ys, dxs = [], []
            for e in range(2):
                head = 2 * pair + e
                ls = weights_of(head, cum, cum_t, step_t)
                m = gram * ls
                mb = m.astype(BF16)
                ge = jnp.where(first if e == 0 else ~first, gp, jnp.zeros_like(gp))
                dm = mm(ge, xp, 1, 1)
                dgram = dgram + dm * ls
                wm = dm * m
                row_sums = jnp.where(lane == head, jnp.sum(wm, axis=1, keepdims=True), row_sums)
                col_sums = jnp.where(sub == head, jnp.sum(wm, axis=0, keepdims=True), col_sums)
                ys.append(mm(mb, xp))
                dxs.append(mm(mb, gp, 0, 0))
            skip = jnp.where(
                lane1 < LANES // 2, skip_ref[base + 2 * pair], skip_ref[base + 2 * pair + 1]
            )
            y = jnp.where(first, ys[0], ys[1]) + skip * xp.astype(F32)
            dx = jnp.where(first, dxs[0], dxs[1]) + skip * gp.astype(F32)
            mixed_ref[:, sl, at : at + LANES] = y.astype(BF16).reshape(frames, group, LANES)
            dx_ref[:, sl, at : at + LANES] = dx.astype(BF16).reshape(frames, group, LANES)
        draw = step_grad(row_sums, col_sums, raw, step, decay_row, mask)
        placed = mm(draw.astype(BF16), pick, 1, 1)
        dgb = (dgram * mask).astype(BF16)
        shape = lambda v: v.astype(BF16).reshape(frames, group, v.shape[1])
        daux_ref[:, sl, :n] = shape(mm(dgb, c, 0, 0))
        daux_ref[:, sl, n : 2 * n] = shape(mm(dgb, b))
        daux_ref[:, sl, 2 * n :] = shape(placed)
    mixed = mixed_ref[...].reshape(frames * patches, width)
    part_ref[...] = mm(mixed, w).astype(BF16).reshape(part_ref.shape)

    @pl.when(pl.program_id(0) == 0)
    def _():
        gw_ref[...] = jnp.zeros_like(gw_ref)

    gw_ref[...] += mm(mixed, go, 0, 0)


VMEM = pl.BlockSpec(memory_space=pltpu.VMEM)
SMEM = pl.BlockSpec(memory_space=pltpu.SMEM)
PARAMS = pltpu.CompilerParams(vmem_limit_bytes=48 * 1024 * 1024)


def on_device(x_inner, bc_inputs, step_raw, decay_rate, skip_gain, w_out, grad_out, tm):
    nheads = skip_gain.shape[0]
    _, patches, inner = x_inner.shape
    n2 = bc_inputs.shape[2] // 2
    model = w_out.shape[1]
    chunk = inner // tm
    mine = nheads // tm
    x, bc, raw = x_inner[0], bc_inputs[0], step_raw[0]
    decay_pad = jnp.pad(decay_rate, ((0, 0), (0, LANES - nheads)))
    aux = jnp.concatenate([bc[:, n2:], raw[:, nheads:]], axis=1)
    aux_all = lax.all_gather(aux, "tm", axis=0)
    go_all = lax.all_gather(grad_out[0], "tm", axis=0)

    spatial = pl.pallas_call(
        functools.partial(forward_kernel, nheads, chunk),
        out_shape=jax.ShapeDtypeStruct((tm, patches, chunk), BF16),
        in_specs=[VMEM] * 4,
        out_specs=VMEM,
        compiler_params=PARAMS,
        name="spatial_forward",
        cost_estimate=pl.CostEstimate(
            flops=6 * patches * patches * inner, bytes_accessed=4 * patches * inner,
            transcendentals=patches * patches * nheads,
        ),
    )(x, bc, raw, decay_pad)
    spatial_here = lax.all_to_all(spatial, "tm", 0, 0, tiled=True)

    rows = 32
    block = lambda width: pl.BlockSpec((tm, rows, width), lambda i: (0, i, 0))
    whole = pl.BlockSpec((chunk, model), lambda i: (0, 0))
    auxw = aux.shape[1]
    base = (lax.axis_index("tm") * mine).astype(jnp.int32).reshape(1)
    grad_here, partial_out, partial_aux, grad_w = pl.pallas_call(
        functools.partial(temporal_kernel, nheads, mine, 16),
        grid=(patches // rows,),
        out_shape=(
            jax.ShapeDtypeStruct((tm, patches, chunk), BF16),
            jax.ShapeDtypeStruct((tm, patches, model), BF16),
            jax.ShapeDtypeStruct((tm, patches, auxw), BF16),
            jax.ShapeDtypeStruct((chunk, model), F32),
        ),
        in_specs=[SMEM, SMEM, SMEM, block(chunk), block(model), block(auxw), whole],
        out_specs=(block(chunk), block(model), block(auxw), whole),
        scratch_shapes=[pltpu.VMEM((tm, rows, chunk), BF16)],
        compiler_params=PARAMS,
        name="temporal",
        cost_estimate=pl.CostEstimate(
            flops=6 * tm * patches * chunk * model, bytes_accessed=8 * tm * patches * model,
            transcendentals=tm * patches * 128 * mine,
        ),
    )(base, decay_rate, skip_gain, spatial_here, go_all, aux_all, w_out)

    grad_spatial = lax.all_to_all(grad_here, "tm", 0, 0, tiled=True)
    mixed_out = lax.psum_scatter(partial_out, "tm", scatter_dimension=0, tiled=True)
    aux_back = lax.psum_scatter(partial_aux, "tm", scatter_dimension=0, tiled=True)[0]

    grad_x, grad_bc_s, grad_raw_s = pl.pallas_call(
        functools.partial(backward_kernel, nheads, chunk),
        out_shape=(
            jax.ShapeDtypeStruct((patches, inner), BF16),
            jax.ShapeDtypeStruct((patches, n2), BF16),
            jax.ShapeDtypeStruct((patches, nheads), BF16),
        ),
        in_specs=[VMEM] * 5,
        out_specs=(VMEM, VMEM, VMEM),
        compiler_params=PARAMS,
        name="spatial_backward",
        cost_estimate=pl.CostEstimate(
            flops=12 * patches * patches * inner, bytes_accessed=6 * patches * inner,
            transcendentals=patches * patches * nheads,
        ),
    )(x, bc, raw, decay_pad, grad_spatial)
    grad_bc = jnp.concatenate([grad_bc_s, aux_back[:, :n2]], axis=1)
    grad_step = jnp.concatenate([grad_raw_s, aux_back[:, n2:]], axis=1)
    return (mixed_out, grad_x[None], grad_bc[None], grad_step[None], grad_w)


def solution(mesh):
    in_specs = (
        P(("clip", "tm"), None, None),
        P(("clip", "tm"), None, None),
        P(("clip", "tm"), None, None),
        P(),
        P(),
        P("tm", None),
        P(("clip", "tm"), None, None),
    )
    out_specs = (
        P(("clip", "tm"), None, None),
        P(("clip", "tm"), None, None),
        P(("clip", "tm"), None, None),
        P(("clip", "tm"), None, None),
        P(("clip", "tm"), None),
    )
    return jax.shard_map(
        functools.partial(on_device, tm=mesh.shape["tm"]),
        mesh=mesh, in_specs=in_specs, out_specs=out_specs, check_vma=False,
    )
```

```python
import functools

import jax
import jax.numpy as jnp
from jax import lax
from jax.experimental import pallas as pl
from jax.experimental.pallas import tpu as pltpu
from jax.sharding import PartitionSpec as P

F32 = jnp.float32
BF16 = jnp.bfloat16
HIGH = lax.Precision.HIGHEST
LANES = 128


def iota(shape, dim):
    return lax.broadcasted_iota(jnp.int32, shape, dim)


def mm(a, b, ca=1, cb=0, precision=None):
    return lax.dot_general(
        a, b, (((ca,), (cb,)), ((), ())), precision=precision, preferred_element_type=F32
    )


def softplus(raw):
    return jnp.maximum(raw, 0.0) + jnp.log(1.0 + jnp.exp(-jnp.abs(raw)))


DMA = pltpu.SemaphoreType.DMA


def picker(rows, base, count):
    r, c = iota((rows, LANES), 0), iota((rows, LANES), 1)
    return jnp.where((r == c + base) & (c < count), 1.0, 0.0).astype(BF16)


def steps_of(raw_bf, pick, decay_row, mask):
    raw = mm(raw_bf, pick)
    step = softplus(raw)
    cum = mm(mask, -step * decay_row, precision=HIGH)
    return raw, step, cum, step.T, cum.T


def weights_of(head, cum, cum_t, step_t):
    gap = cum[:, head : head + 1] - cum_t[head : head + 1, :]
    return jnp.exp(jnp.minimum(gap, 0.0)) * step_t[head : head + 1, :]


def step_grad(row_sums, col_sums_t, raw, step, decay_row, mask):
    col_sums = col_sums_t.T
    later = mm(mask, row_sums - col_sums, 0, 0, precision=HIGH)
    grad = col_sums / step - decay_row * later
    return grad / (1.0 + jnp.exp(-raw))


def remote(src, dst, send, recv, peer):
    return pltpu.make_async_remote_copy(
        src_ref=src, dst_ref=dst, send_sem=send, recv_sem=recv,
        device_id={"tm": peer}, device_id_type=pl.DeviceIdType.MESH,
    )


def greet_all(me, tm):
    barrier = pltpu.get_barrier_semaphore()
    for d in range(1, tm):
        pl.semaphore_signal(
            barrier, inc=1, device_id={"tm": lax.rem(me + d, tm)},
            device_id_type=pl.DeviceIdType.MESH,
        )
    pl.semaphore_wait(barrier, tm - 1)


def forward_kernel(
    nheads, chunk, tm,
    x_ref, bc_ref, raw_ref, decay_ref, go_ref, aux_ref,
    here_ref, go_all, aux_all,
    out_ref, own_sem, sp_send, sp_recv, go_send, go_recv, aux_send, aux_recv,
):
    length = x_ref.shape[0]
    n = bc_ref.shape[1] // 4
    me = lax.axis_index("tm")
    core = lax.rem(me, 2)
    partner = me + 1 - 2 * core
    own = [
        pltpu.make_async_copy(go_ref, go_all.at[me], own_sem.at[0]),
        pltpu.make_async_copy(aux_ref, aux_all.at[me], own_sem.at[1]),
    ]
    for copy in own:
        copy.start()
    greet_all(me, tm)
    gathers = ((go_ref, go_all, go_send, go_recv), (aux_ref, aux_all, aux_send, aux_recv))
    sends = []
    for src, dst, send, recv in gathers:
        for d in range(tm // 2):
            peer = partner if d == 0 else lax.rem(me + 2 * d, tm)
            sends.append(remote(src, dst.at[me], send.at[d], recv.at[me], peer))
            sends[-1].start()

    mask = jnp.where(iota((length, length), 0) >= iota((length, length), 1), 1.0, 0.0)
    pick = picker(raw_ref.shape[1], 0, nheads)
    _, _, cum, step_t, cum_t = steps_of(raw_ref[...], pick, decay_ref[0:1, :], mask)
    gram = mm(bc_ref[:, n : 2 * n], bc_ref[:, :n], 1, 1) * mask
    first = iota((length, LANES), 1) < LANES // 2
    for pair in range(nheads // 2):
        xp = x_ref[:, pair * LANES : (pair + 1) * LANES]
        ys = []
        for e in range(2):
            m = gram * weights_of(2 * pair + e, cum, cum_t, step_t)
            ys.append(mm(m.astype(BF16), xp))
        at = pair * LANES
        out_ref[at // chunk, :, at % chunk : at % chunk + LANES] = jnp.where(
            first, ys[0], ys[1]
        ).astype(BF16)

    own.append(pltpu.make_async_copy(out_ref.at[me], here_ref.at[me], own_sem.at[2]))
    own[-1].start()
    for d in range(1, tm):
        peer = lax.rem(me + d, tm)
        sends.append(
            remote(out_ref.at[peer], here_ref.at[me], sp_send.at[d], sp_recv.at[me], peer)
        )
        sends[-1].start()
    for src, dst, send, recv in reversed(gathers):
        for d in range(1, tm // 2):
            got = lax.rem(me + 2 * d, tm)
            remote(src, dst.at[got], send.at[0], recv.at[got], partner).wait_recv()
            sends.append(
                remote(dst.at[got], dst.at[got], send.at[tm // 2 + d], recv.at[got], partner)
            )
            sends[-1].start()
    for src, dst, send, recv in gathers:
        for d in range(tm // 2):
            got = lax.rem(partner + 2 * d, tm)
            remote(src, dst.at[got], send.at[0], recv.at[got], partner).wait_recv()
    for d in range(1, tm):
        got = lax.rem(me + d, tm)
        remote(out_ref.at[got], here_ref.at[got], sp_send.at[d], sp_recv.at[got], got).wait_recv()
    for copy in own:
        copy.wait()
    for copy in sends:
        copy.wait_send()


def backward_kernel(
    nheads, chunk, tm,
    x_ref, bc_ref, raw_ref, decay_ref, grad_ref, part_ref, paux_ref,
    dx_ref, dbc_ref, draw_ref, out_ref,
    dy_ref, own_part, own_aux, in_part, in_aux, sum_part, sum_aux, far_part, far_aux,
    own_sem, dy_send, dy_recv, near_send, near_recv, far_send, far_recv,
):
    chips = tm // 2
    me = lax.axis_index("tm")
    core = lax.rem(me, 2)
    chip = lax.div(me, 2)
    partner = me + 1 - 2 * core
    own = [pltpu.make_async_copy(grad_ref.at[me], dy_ref.at[me], own_sem.at[0, 0])]
    kinds = (
        (part_ref, own_part, in_part, sum_part, far_part),
        (paux_ref, own_aux, in_aux, sum_aux, far_aux),
    )
    for k, (src, mine, _, _, _) in enumerate(kinds):
        for q in range(chips):
            own.append(pltpu.make_async_copy(src.at[2 * q + core], mine.at[q], own_sem.at[k + 1, q]))
    for copy in own:
        copy.start()
    greet_all(me, tm)
    sends, nears = [], []
    for k, (src, _, near, _, _) in enumerate(kinds):
        for q in range(chips):
            nears.append(
                remote(
                    src.at[2 * q + 1 - core], near.at[q], near_send.at[k, q], near_recv.at[k, q],
                    partner,
                )
            )
            nears[-1].start()
    for d in range(1, tm):
        peer = lax.rem(me + d, tm)
        sends.append(
            remote(grad_ref.at[peer], dy_ref.at[me], dy_send.at[d], dy_recv.at[me], peer)
        )
        sends[-1].start()
    for copy in own + nears:
        copy.wait()
    for k, (_, mine, near, total, far) in enumerate(kinds):
        for d in range(1, chips):
            q = lax.rem(chip + d, chips)
            total[q] = (mine[q].astype(F32) + near[q].astype(F32)).astype(BF16)
            sends.append(
                remote(
                    total.at[q], far.at[chip], far_send.at[k, d], far_recv.at[k, chip],
                    2 * q + core,
                )
            )
            sends[-1].start()
    for d in range(1, tm):
        got = lax.rem(me + d, tm)
        remote(grad_ref.at[got], dy_ref.at[got], dy_send.at[d], dy_recv.at[got], got).wait_recv()

    length = x_ref.shape[0]
    n = bc_ref.shape[1] // 4
    mask = jnp.where(iota((length, length), 0) >= iota((length, length), 1), 1.0, 0.0)
    pick = picker(raw_ref.shape[1], 0, nheads)
    decay_row = decay_ref[0:1, :]
    raw, step, cum, step_t, cum_t = steps_of(raw_ref[...], pick, decay_row, mask)
    b, c = bc_ref[:, :n], bc_ref[:, n : 2 * n]
    gram = mm(c, b, 1, 1) * mask
    lane = iota((length, LANES), 1)
    first = lane < LANES // 2
    sub = iota((LANES, length), 0)
    dgram = jnp.zeros((length, length), F32)
    row_sums = jnp.zeros((length, LANES), F32)
    col_sums = jnp.zeros((LANES, length), F32)
    for pair in range(nheads // 2):
        at = pair * LANES
        xp = x_ref[:, at : at + LANES]
        gp = dy_ref[at // chunk, :, at % chunk : at % chunk + LANES]
        dxs = []
        for e in range(2):
            head = 2 * pair + e
            ls = weights_of(head, cum, cum_t, step_t)
            m = gram * ls
            ge = jnp.where(first if e == 0 else ~first, gp, jnp.zeros_like(gp))
            dm = mm(ge, xp, 1, 1)
            dgram = dgram + dm * ls
            w = dm * m
            row_sums = jnp.where(lane == head, jnp.sum(w, axis=1, keepdims=True), row_sums)
            col_sums = jnp.where(sub == head, jnp.sum(w, axis=0, keepdims=True), col_sums)
            dxs.append(mm(m.astype(BF16), gp, 0, 0))
        dx_ref[:, at : at + LANES] = jnp.where(first, dxs[0], dxs[1]).astype(BF16)
    draw = step_grad(row_sums, col_sums, raw, step, decay_row, mask)
    draw_ref[:, :nheads] = draw[:, :nheads].astype(BF16)
    dgb = (dgram * mask).astype(BF16)
    dbc_ref[:, :n] = mm(dgb, c, 0, 0).astype(BF16)
    dbc_ref[:, n : 2 * n] = mm(dgb, b).astype(BF16)

    totals = []
    for k, (_, mine, near, total, far) in enumerate(kinds):
        value = mine[chip].astype(F32) + near[chip].astype(F32)
        for d in range(1, chips):
            q = lax.rem(chip + d, chips)
            remote(
                total.at[q], far.at[q], far_send.at[k, d], far_recv.at[k, q], 2 * q + core
            ).wait_recv()
            value = value + far[q].astype(F32)
        totals.append(value.astype(BF16))
    out_ref[...] = totals[0]
    dbc_ref[:, 2 * n :] = totals[1][:, : 2 * n]
    draw_ref[:, nheads:] = totals[1][:, 2 * n :]
    for copy in sends:
        copy.wait_send()


def temporal_kernel(
    nheads, mine, group,
    base_ref, decay_ref, skip_ref, x_ref, go_ref, aux_ref, w_ref,
    dx_ref, part_ref, daux_ref, gw_ref, mixed_ref,
):
    frames, patches, width = x_ref.shape
    n = (aux_ref.shape[2] - nheads) // 2
    base = base_ref[0]
    rows = frames * group
    ri, ci = iota((rows, rows), 0), iota((rows, rows), 1)
    mask = jnp.where((ri % group == ci % group) & (ri >= ci), 1.0, 0.0)
    pick = picker(nheads, base, mine)
    lane = iota((rows, LANES), 1)
    sub = iota((LANES, rows), 0)
    first = lane < LANES // 2
    lane1 = iota((1, LANES), 1)
    decay_row = jnp.zeros((1, LANES), F32)
    for h in range(mine):
        decay_row = jnp.where(lane1 == h, decay_ref[1, base + h], decay_row)
    w = w_ref[...]
    go = go_ref[...].reshape(frames * patches, go_ref.shape[2])
    carried = mm(go, w, 1, 1).astype(BF16).reshape(frames, patches, width)
    for part in range(patches // group):
        sl = slice(part * group, (part + 1) * group)
        x = x_ref[:, sl, :].reshape(rows, width)
        g = carried[:, sl, :].reshape(rows, width)
        aux = aux_ref[:, sl, :].reshape(rows, aux_ref.shape[2])
        b, c = aux[:, :n], aux[:, n : 2 * n]
        raw, step, cum, step_t, cum_t = steps_of(aux[:, 2 * n :], pick, decay_row, mask)
        gram = mm(c, b, 1, 1) * mask
        dgram = jnp.zeros((rows, rows), F32)
        row_sums = jnp.zeros((rows, LANES), F32)
        col_sums = jnp.zeros((LANES, rows), F32)
        for pair in range(mine // 2):
            at = pair * LANES
            xp, gp = x[:, at : at + LANES], g[:, at : at + LANES]
            ys, dxs = [], []
            for e in range(2):
                head = 2 * pair + e
                ls = weights_of(head, cum, cum_t, step_t)
                m = gram * ls
                mb = m.astype(BF16)
                ge = jnp.where(first if e == 0 else ~first, gp, jnp.zeros_like(gp))
                dm = mm(ge, xp, 1, 1)
                dgram = dgram + dm * ls
                wm = dm * m
                row_sums = jnp.where(lane == head, jnp.sum(wm, axis=1, keepdims=True), row_sums)
                col_sums = jnp.where(sub == head, jnp.sum(wm, axis=0, keepdims=True), col_sums)
                ys.append(mm(mb, xp))
                dxs.append(mm(mb, gp, 0, 0))
            skip = jnp.where(
                lane1 < LANES // 2, skip_ref[base + 2 * pair], skip_ref[base + 2 * pair + 1]
            )
            y = jnp.where(first, ys[0], ys[1]) + skip * xp.astype(F32)
            dx = jnp.where(first, dxs[0], dxs[1]) + skip * gp.astype(F32)
            mixed_ref[:, sl, at : at + LANES] = y.astype(BF16).reshape(frames, group, LANES)
            dx_ref[:, sl, at : at + LANES] = dx.astype(BF16).reshape(frames, group, LANES)
        draw = step_grad(row_sums, col_sums, raw, step, decay_row, mask)
        placed = mm(draw.astype(BF16), pick, 1, 1)
        dgb = (dgram * mask).astype(BF16)
        shape = lambda v: v.astype(BF16).reshape(frames, group, v.shape[1])
        daux_ref[:, sl, :n] = shape(mm(dgb, c, 0, 0))
        daux_ref[:, sl, n : 2 * n] = shape(mm(dgb, b))
        daux_ref[:, sl, 2 * n :] = shape(placed)
    mixed = mixed_ref[...].reshape(frames * patches, width)
    part_ref[...] = mm(mixed, w).astype(BF16).reshape(part_ref.shape)

    @pl.when(pl.program_id(0) == 0)
    def _():
        gw_ref[...] = jnp.zeros_like(gw_ref)

    gw_ref[...] += mm(mixed, go, 0, 0)


VMEM = pl.BlockSpec(memory_space=pltpu.VMEM)
ANY = pl.BlockSpec(memory_space=pl.ANY)
SMEM = pl.BlockSpec(memory_space=pltpu.SMEM)
LIMIT = 48 * 1024 * 1024
PARAMS = pltpu.CompilerParams(vmem_limit_bytes=LIMIT)


def talking(number):
    return pltpu.CompilerParams(
        vmem_limit_bytes=LIMIT, collective_id=number, has_side_effects=True
    )


def on_device(x_inner, bc_inputs, step_raw, decay_rate, skip_gain, w_out, grad_out, tm):
    nheads = skip_gain.shape[0]
    _, patches, inner = x_inner.shape
    n2 = bc_inputs.shape[2] // 2
    model = w_out.shape[1]
    chunk = inner // tm
    mine = nheads // tm
    x, bc, raw = x_inner[0], bc_inputs[0], step_raw[0]
    decay_pad = jnp.pad(decay_rate, ((0, 0), (0, LANES - nheads)))
    aux = jnp.concatenate([bc[:, n2:], raw[:, nheads:]], axis=1)
    auxw = aux.shape[1]

    spatial_here, go_all, aux_all = pl.pallas_call(
        functools.partial(forward_kernel, nheads, chunk, tm),
        out_shape=(
            jax.ShapeDtypeStruct((tm, patches, chunk), BF16),
            jax.ShapeDtypeStruct((tm, patches, model), BF16),
            jax.ShapeDtypeStruct((tm, patches, auxw), BF16),
        ),
        in_specs=[VMEM] * 4 + [ANY] * 2,
        out_specs=(ANY, ANY, ANY),
        scratch_shapes=[pltpu.VMEM((tm, patches, chunk), BF16), DMA((3,))] + [DMA((tm,))] * 6,
        compiler_params=talking(0),
        name="spatial_forward",
        cost_estimate=pl.CostEstimate(
            flops=6 * patches * patches * inner, bytes_accessed=4 * patches * inner,
            transcendentals=patches * patches * nheads,
        ),
    )(x, bc, raw, decay_pad, grad_out[0], aux)

    rows = 32
    block = lambda width: pl.BlockSpec((tm, rows, width), lambda i: (0, i, 0))
    whole = pl.BlockSpec((chunk, model), lambda i: (0, 0))
    base = (lax.axis_index("tm") * mine).astype(jnp.int32).reshape(1)
    grad_here, partial_out, partial_aux, grad_w = pl.pallas_call(
        functools.partial(temporal_kernel, nheads, mine, 16),
        grid=(patches // rows,),
        out_shape=(
            jax.ShapeDtypeStruct((tm, patches, chunk), BF16),
            jax.ShapeDtypeStruct((tm, patches, model), BF16),
            jax.ShapeDtypeStruct((tm, patches, auxw), BF16),
            jax.ShapeDtypeStruct((chunk, model), F32),
        ),
        in_specs=[SMEM, SMEM, SMEM, block(chunk), block(model), block(auxw), whole],
        out_specs=(block(chunk), block(model), block(auxw), whole),
        scratch_shapes=[pltpu.VMEM((tm, rows, chunk), BF16)],
        compiler_params=PARAMS,
        name="temporal",
        cost_estimate=pl.CostEstimate(
            flops=6 * tm * patches * chunk * model, bytes_accessed=8 * tm * patches * model,
            transcendentals=tm * patches * 128 * mine,
        ),
    )(base, decay_rate, skip_gain, spatial_here, go_all, aux_all, w_out)

    chips = tm // 2
    slots = lambda width: pltpu.VMEM((chips, patches, width), BF16)
    grad_x, grad_bc, grad_step, mixed_out = pl.pallas_call(
        functools.partial(backward_kernel, nheads, chunk, tm),
        out_shape=(
            jax.ShapeDtypeStruct((patches, inner), BF16),
            jax.ShapeDtypeStruct((patches, 2 * n2), BF16),
            jax.ShapeDtypeStruct((patches, 2 * nheads), BF16),
            jax.ShapeDtypeStruct((patches, model), BF16),
        ),
        in_specs=[VMEM] * 4 + [ANY] * 3,
        out_specs=(VMEM,) * 4,
        scratch_shapes=[pltpu.VMEM((tm, patches, chunk), BF16)]
        + [slots(model), slots(auxw)] * 4
        + [DMA((3, chips)), DMA((tm,)), DMA((tm,))]
        + [DMA((2, chips))] * 4,
        compiler_params=talking(1),
        name="spatial_backward",
        cost_estimate=pl.CostEstimate(
            flops=12 * patches * patches * inner, bytes_accessed=6 * patches * inner,
            transcendentals=patches * patches * nheads,
        ),
    )(x, bc, raw, decay_pad, grad_here, partial_out, partial_aux)
    return (mixed_out[None], grad_x[None], grad_bc[None], grad_step[None], grad_w)


def solution(mesh):
    in_specs = (
        P(("clip", "tm"), None, None),
        P(("clip", "tm"), None, None),
        P(("clip", "tm"), None, None),
        P(),
        P(),
        P("tm", None),
        P(("clip", "tm"), None, None),
    )
    out_specs = (
        P(("clip", "tm"), None, None),
        P(("clip", "tm"), None, None),
        P(("clip", "tm"), None, None),
        P(("clip", "tm"), None, None),
        P(("clip", "tm"), None),
    )
    return jax.shard_map(
        functools.partial(on_device, tm=mesh.shape["tm"]),
        mesh=mesh, in_specs=in_specs, out_specs=out_specs, check_vma=False,
    )
```

```python
import functools

import jax
import jax.numpy as jnp
from jax import lax
from jax.experimental import pallas as pl
from jax.experimental.pallas import tpu as pltpu
from jax.sharding import PartitionSpec as P

F32 = jnp.float32
BF16 = jnp.bfloat16
HIGH = lax.Precision.HIGHEST
LANES = 128


def iota(shape, dim):
    return lax.broadcasted_iota(jnp.int32, shape, dim)


def mm(a, b, ca=1, cb=0, precision=None):
    return lax.dot_general(
        a, b, (((ca,), (cb,)), ((), ())), precision=precision, preferred_element_type=F32
    )


def softplus(raw):
    return jnp.maximum(raw, 0.0) + jnp.log(1.0 + jnp.exp(-jnp.abs(raw)))


DMA = pltpu.SemaphoreType.DMA


def picker(rows, base, count):
    r, c = iota((rows, LANES), 0), iota((rows, LANES), 1)
    return jnp.where((r == c + base) & (c < count), 1.0, 0.0).astype(BF16)


def decay_lanes(decay_ref):
    row = decay_ref[0:1, :]
    return jnp.concatenate([row, jnp.zeros((1, LANES - row.shape[1]), F32)], axis=1)


def steps_of(raw_bf, pick, decay_row, mask):
    raw = mm(raw_bf, pick)
    step = softplus(raw)
    cum = mm(mask, -step * decay_row, precision=HIGH)
    return raw, step, cum, step.T, cum.T


def weights_of(head, cum, cum_t, step_t):
    gap = cum[:, head : head + 1] - cum_t[head : head + 1, :]
    return jnp.exp(jnp.minimum(gap, 0.0)) * step_t[head : head + 1, :]


def step_grad(row_sums, col_sums_t, raw, step, decay_row, mask):
    col_sums = col_sums_t.T
    later = mm(mask, row_sums - col_sums, 0, 0, precision=HIGH)
    grad = col_sums / step - decay_row * later
    return grad / (1.0 + jnp.exp(-raw))


def remote(src, dst, send, recv, peer):
    return pltpu.make_async_remote_copy(
        src_ref=src, dst_ref=dst, send_sem=send, recv_sem=recv,
        device_id={"tm": peer}, device_id_type=pl.DeviceIdType.MESH,
    )


def greet_all(me, tm):
    barrier = pltpu.get_barrier_semaphore()
    for d in range(1, tm):
        pl.semaphore_signal(
            barrier, inc=1, device_id={"tm": lax.rem(me + d, tm)},
            device_id_type=pl.DeviceIdType.MESH,
        )
    pl.semaphore_wait(barrier, tm - 1)


def forward_kernel(
    nheads, chunk, tm,
    x_ref, bc_ref, raw_ref, decay_ref, go_ref,
    here_ref, go_all, aux_all,
    out_ref, aux_vm, own_sem, sp_send, sp_recv, go_send, go_recv, aux_send, aux_recv,
):
    length = x_ref.shape[0]
    n = bc_ref.shape[1] // 4
    me = lax.axis_index("tm")
    core = lax.rem(me, 2)
    partner = me + 1 - 2 * core
    chips, chip = tm // 2, lax.div(me, 2)
    aux_vm[:, : 2 * n] = bc_ref[:, 2 * n :]
    aux_vm[:, 2 * n :] = raw_ref[:, nheads:]
    own = [
        pltpu.make_async_copy(go_ref, go_all.at[me], own_sem.at[0]),
        pltpu.make_async_copy(aux_vm, aux_all.at[me], own_sem.at[1]),
    ]
    for copy in own:
        copy.start()
    greet_all(me, tm)
    gathers = ((aux_vm, aux_all, aux_send, aux_recv), (go_ref, go_all, go_send, go_recv))

    def hand_on(src, dst, send, recv, owner, right, left):
        @pl.when(right)
        def _():
            remote(src, dst.at[owner], send.at[0, owner], recv.at[owner], me + 2).start()

        @pl.when(left)
        def _():
            remote(src, dst.at[owner], send.at[1, owner], recv.at[owner], me - 2).start()

        remote(src, dst.at[owner], send.at[2, owner], recv.at[owner], partner).start()

    for src, dst, send, recv in gathers:
        hand_on(src, dst, send, recv, me, chip < chips - 1, chip > 0)

    mask = jnp.where(iota((length, length), 0) >= iota((length, length), 1), 1.0, 0.0)
    pick = picker(raw_ref.shape[1], 0, nheads)
    _, _, cum, step_t, cum_t = steps_of(raw_ref[...], pick, decay_lanes(decay_ref), mask)
    gram = mm(bc_ref[:, n : 2 * n], bc_ref[:, :n], 1, 1) * mask
    first = iota((length, LANES), 1) < LANES // 2
    for pair in range(nheads // 2):
        xp = x_ref[:, pair * LANES : (pair + 1) * LANES]
        ys = []
        for e in range(2):
            m = gram * weights_of(2 * pair + e, cum, cum_t, step_t)
            ys.append(mm(m.astype(BF16), xp))
        at = pair * LANES
        out_ref[at // chunk, :, at % chunk : at % chunk + LANES] = jnp.where(
            first, ys[0], ys[1]
        ).astype(BF16)

    sends = []
    own.append(pltpu.make_async_copy(out_ref.at[me], here_ref.at[me], own_sem.at[2]))
    own[-1].start()
    for d in range(1, tm):
        peer = lax.rem(me + d, tm)
        sends.append(
            remote(out_ref.at[peer], here_ref.at[me], sp_send.at[d], sp_recv.at[me], peer)
        )
        sends[-1].start()
    def passing(step, wait):
        for sign in (-1, 1):
            got = me + 2 * sign * step
            here = (chip >= step) if sign < 0 else (chip < chips - step)
            right = (chip < chips - 1) if sign < 0 else (chip < 0)
            left = (chip < 0) if sign < 0 else (chip > 0)

            @pl.when(here)
            def _():
                for src, dst, send, recv in gathers:
                    wait(src, dst, send, recv, got, right, left)

    def take(src, dst, send, recv, got, right, left):
        remote(src, dst.at[got], send.at[2, got], recv.at[got], partner).wait_recv()
        hand_on(dst.at[got], dst, send, recv, got, right, left)

    def sent(src, dst, send, recv, got, right, left):
        @pl.when(right)
        def _():
            remote(src, dst.at[got], send.at[0, got], recv.at[got], me + 2).wait_send()

        @pl.when(left)
        def _():
            remote(src, dst.at[got], send.at[1, got], recv.at[got], me - 2).wait_send()

        remote(src, dst.at[got], send.at[2, got], recv.at[got], partner).wait_send()

    for step in range(1, chips):
        passing(step, take)
    for src, dst, send, recv in gathers:
        for d in range(chips):
            got = lax.rem(partner + 2 * d, tm)
            remote(src, dst.at[got], send.at[2, got], recv.at[got], partner).wait_recv()
    for d in range(1, tm):
        got = lax.rem(me + d, tm)
        remote(out_ref.at[got], here_ref.at[got], sp_send.at[d], sp_recv.at[got], got).wait_recv()
    for copy in own:
        copy.wait()
    for copy in sends:
        copy.wait_send()
    for src, dst, send, recv in gathers:
        sent(src, dst, send, recv, me, chip < chips - 1, chip > 0)
    for step in range(1, chips):
        passing(step, sent)


def backward_kernel(
    nheads, chunk, tm,
    x_ref, bc_ref, raw_ref, decay_ref, grad_ref, part_ref, paux_ref,
    dx_ref, dbc_ref, draw_ref, out_ref,
    dy_ref, own_part, own_aux, in_part, in_aux, sum_part, sum_aux, far_part, far_aux,
    own_sem, dy_send, dy_recv, near_send, near_recv, far_send, far_recv,
):
    chips = tm // 2
    me = lax.axis_index("tm")
    core = lax.rem(me, 2)
    chip = lax.div(me, 2)
    partner = me + 1 - 2 * core
    own = [pltpu.make_async_copy(grad_ref.at[me], dy_ref.at[me], own_sem.at[0, 0])]
    kinds = (
        (part_ref, own_part, in_part, sum_part, far_part),
        (paux_ref, own_aux, in_aux, sum_aux, far_aux),
    )
    for k, (src, mine, _, _, _) in enumerate(kinds):
        for q in range(chips):
            own.append(pltpu.make_async_copy(src.at[2 * q + core], mine.at[q], own_sem.at[k + 1, q]))
    for copy in own:
        copy.start()
    greet_all(me, tm)
    sends, nears = [], []
    for k, (src, _, near, _, _) in enumerate(kinds):
        for q in range(chips):
            nears.append(
                remote(
                    src.at[2 * q + 1 - core], near.at[q], near_send.at[k, q], near_recv.at[k, q],
                    partner,
                )
            )
            nears[-1].start()
    for d in range(1, tm):
        peer = lax.rem(me + d, tm)
        sends.append(
            remote(grad_ref.at[peer], dy_ref.at[me], dy_send.at[d], dy_recv.at[me], peer)
        )
        sends[-1].start()
    for copy in own + nears:
        copy.wait()

    def hop(k, q, side):
        total, far = kinds[k][3], kinds[k][4]
        return remote(
            total.at[q], far.at[side, q], far_send.at[k, q], far_recv.at[k, side, q],
            lax.rem(me + tm + 2 - 4 * side, tm),
        )

    def forward(q, side):
        for k, (_, mine, near, total, far) in reversed(list(enumerate(kinds))):
            total[q] = (mine[q].astype(F32) + near[q].astype(F32)).astype(BF16)

            @pl.when((chip > 0) if side == 0 else (chip < chips - 1))
            def _():
                hop(k, q, side).wait_recv()
                total[q] = (
                    mine[q].astype(F32) + near[q].astype(F32) + far[side, q].astype(F32)
                ).astype(BF16)

            hop(k, q, side).start()

    def round_of(step):
        @pl.when(chips - 1 - step > chip)
        def _():
            forward(chips - 1 - step, 0)

        @pl.when(step < chip)
        def _():
            forward(step, 1)

    round_of(0)
    for d in range(1, tm):
        got = lax.rem(me + d, tm)
        remote(grad_ref.at[got], dy_ref.at[got], dy_send.at[d], dy_recv.at[got], got).wait_recv()

    length = x_ref.shape[0]
    n = bc_ref.shape[1] // 4
    mask = jnp.where(iota((length, length), 0) >= iota((length, length), 1), 1.0, 0.0)
    pick = picker(raw_ref.shape[1], 0, nheads)
    decay_row = decay_lanes(decay_ref)
    raw, step, cum, step_t, cum_t = steps_of(raw_ref[...], pick, decay_row, mask)
    b, c = bc_ref[:, :n], bc_ref[:, n : 2 * n]
    gram = mm(c, b, 1, 1) * mask
    lane = iota((length, LANES), 1)
    first = lane < LANES // 2
    sub = iota((LANES, length), 0)
    dgram = jnp.zeros((length, length), F32)
    row_sums = jnp.zeros((length, LANES), F32)
    col_sums = jnp.zeros((LANES, length), F32)
    for pair in range(nheads // 2):
        if pair and pair % (nheads // 2 // (chips - 1) + 1) == 0:
            round_of(pair // (nheads // 2 // (chips - 1) + 1))
        at = pair * LANES
        xp = x_ref[:, at : at + LANES]
        gp = dy_ref[at // chunk, :, at % chunk : at % chunk + LANES]
        dxs = []
        for e in range(2):
            head = 2 * pair + e
            ls = weights_of(head, cum, cum_t, step_t)
            m = gram * ls
            ge = jnp.where(first if e == 0 else ~first, gp, jnp.zeros_like(gp))
            dm = mm(ge, xp, 1, 1)
            dgram = dgram + dm * ls
            w = dm * m
            row_sums = jnp.where(lane == head, jnp.sum(w, axis=1, keepdims=True), row_sums)
            col_sums = jnp.where(sub == head, jnp.sum(w, axis=0, keepdims=True), col_sums)
            dxs.append(mm(m.astype(BF16), gp, 0, 0))
        dx_ref[:, at : at + LANES] = jnp.where(first, dxs[0], dxs[1]).astype(BF16)
    draw = step_grad(row_sums, col_sums, raw, step, decay_row, mask)
    draw_ref[:, :nheads] = draw[:, :nheads].astype(BF16)
    dgb = (dgram * mask).astype(BF16)
    dbc_ref[:, :n] = mm(dgb, c, 0, 0).astype(BF16)
    dbc_ref[:, n : 2 * n] = mm(dgb, b).astype(BF16)

    for k, (_, mine, near, total, far) in reversed(list(enumerate(kinds))):
        total[chip] = (mine[chip].astype(F32) + near[chip].astype(F32)).astype(BF16)
        for side in range(2):
            @pl.when((chip > 0) if side == 0 else (chip < chips - 1))
            def _():
                hop(k, chip, side).wait_recv()
                total[chip] = (total[chip].astype(F32) + far[side, chip].astype(F32)).astype(BF16)

    out_ref[...] = sum_part[chip]
    other = sum_aux[chip]
    dbc_ref[:, 2 * n :] = other[:, : 2 * n]
    draw_ref[:, nheads:] = other[:, 2 * n :]
    for copy in sends:
        copy.wait_send()
    for k in range(2):
        for q in range(chips):
            @pl.when(chip != q)
            def _():
                hop(k, q, 0).wait_send()


def temporal_kernel(
    nheads, mine, group,
    base_ref, decay_ref, skip_ref, x_ref, go_ref, aux_ref, w_ref,
    dx_ref, part_ref, daux_ref, gw_ref, mixed_ref,
):
    frames, patches, width = x_ref.shape
    n = (aux_ref.shape[2] - nheads) // 2
    base = base_ref[0]
    rows = frames * group
    ri, ci = iota((rows, rows), 0), iota((rows, rows), 1)
    mask = jnp.where((ri % group == ci % group) & (ri >= ci), 1.0, 0.0)
    pick = picker(nheads, base, mine)
    lane = iota((rows, LANES), 1)
    sub = iota((LANES, rows), 0)
    first = lane < LANES // 2
    lane1 = iota((1, LANES), 1)
    decay_row = jnp.zeros((1, LANES), F32)
    for h in range(mine):
        decay_row = jnp.where(lane1 == h, decay_ref[1, base + h], decay_row)
    w = w_ref[...]
    go = go_ref[...].reshape(frames * patches, go_ref.shape[2])
    carried = mm(go, w, 1, 1).astype(BF16).reshape(frames, patches, width)
    raws = mm(aux_ref[:, :, 2 * n :].reshape(frames * patches, nheads), pick)
    steps = softplus(raws)
    logs = (-steps * decay_row).reshape(frames, patches, LANES)
    raws, steps = (v.reshape(frames, patches, LANES) for v in (raws, steps))
    cums = [logs[0]]
    for f in range(1, frames):
        cums.append(cums[-1] + logs[f])
    cums = jnp.stack(cums)
    for part in range(patches // group):
        sl = slice(part * group, (part + 1) * group)
        x = x_ref[:, sl, :].reshape(rows, width)
        g = carried[:, sl, :].reshape(rows, width)
        aux = aux_ref[:, sl, :].reshape(rows, aux_ref.shape[2])
        b, c = aux[:, :n], aux[:, n : 2 * n]
        raw, step, cum = (v[:, sl, :].reshape(rows, LANES) for v in (raws, steps, cums))
        step_t, cum_t = step.T, cum.T
        gram = mm(c, b, 1, 1) * mask
        dgram = jnp.zeros((rows, rows), F32)
        row_sums = jnp.zeros((rows, LANES), F32)
        col_sums = jnp.zeros((LANES, rows), F32)
        for pair in range(mine // 2):
            at = pair * LANES
            xp, gp = x[:, at : at + LANES], g[:, at : at + LANES]
            ys, dxs = [], []
            for e in range(2):
                head = 2 * pair + e
                ls = weights_of(head, cum, cum_t, step_t)
                m = gram * ls
                mb = m.astype(BF16)
                ge = jnp.where(first if e == 0 else ~first, gp, jnp.zeros_like(gp))
                dm = mm(ge, xp, 1, 1)
                dgram = dgram + dm * ls
                wm = dm * m
                row_sums = jnp.where(lane == head, jnp.sum(wm, axis=1, keepdims=True), row_sums)
                col_sums = jnp.where(sub == head, jnp.sum(wm, axis=0, keepdims=True), col_sums)
                ys.append(mm(mb, xp))
                dxs.append(mm(mb, gp, 0, 0))
            skip = jnp.where(
                lane1 < LANES // 2, skip_ref[base + 2 * pair], skip_ref[base + 2 * pair + 1]
            )
            y = jnp.where(first, ys[0], ys[1]) + skip * xp.astype(F32)
            dx = jnp.where(first, dxs[0], dxs[1]) + skip * gp.astype(F32)
            mixed_ref[:, sl, at : at + LANES] = y.astype(BF16).reshape(frames, group, LANES)
            dx_ref[:, sl, at : at + LANES] = dx.astype(BF16).reshape(frames, group, LANES)
        col_sums = col_sums.T
        ends = (row_sums - col_sums).reshape(frames, group, LANES)
        later = [ends[frames - 1]]
        for f in range(frames - 2, -1, -1):
            later.append(later[-1] + ends[f])
        later = jnp.stack(later[::-1]).reshape(rows, LANES)
        draw = (col_sums / step - decay_row * later) / (1.0 + jnp.exp(-raw))
        placed = mm(draw.astype(BF16), pick, 1, 1)
        dgb = (dgram * mask).astype(BF16)
        shape = lambda v: v.astype(BF16).reshape(frames, group, v.shape[1])
        daux_ref[:, sl, :n] = shape(mm(dgb, c, 0, 0))
        daux_ref[:, sl, n : 2 * n] = shape(mm(dgb, b))
        daux_ref[:, sl, 2 * n :] = shape(placed)
    mixed = mixed_ref[...].reshape(frames * patches, width)
    part_ref[...] = mm(mixed, w).astype(BF16).reshape(part_ref.shape)

    @pl.when(pl.program_id(0) == 0)
    def _():
        gw_ref[...] = jnp.zeros_like(gw_ref)

    gw_ref[...] += mm(mixed, go, 0, 0)


VMEM = pl.BlockSpec(memory_space=pltpu.VMEM)
ANY = pl.BlockSpec(memory_space=pl.ANY)
SMEM = pl.BlockSpec(memory_space=pltpu.SMEM)
LIMIT = 60 * 1024 * 1024
PARAMS = pltpu.CompilerParams(vmem_limit_bytes=LIMIT)


def talking(number):
    return pltpu.CompilerParams(
        vmem_limit_bytes=LIMIT, collective_id=number, has_side_effects=True
    )


def on_device(x_inner, bc_inputs, step_raw, decay_rate, skip_gain, w_out, grad_out, tm):
    nheads = skip_gain.shape[0]
    _, patches, inner = x_inner.shape
    n2 = bc_inputs.shape[2] // 2
    model = w_out.shape[1]
    chunk = inner // tm
    mine = nheads // tm
    x, bc, raw = x_inner[0], bc_inputs[0], step_raw[0]
    auxw = n2 + nheads

    spatial_here, go_all, aux_all = pl.pallas_call(
        functools.partial(forward_kernel, nheads, chunk, tm),
        out_shape=(
            jax.ShapeDtypeStruct((tm, patches, chunk), BF16),
            jax.ShapeDtypeStruct((tm, patches, model), BF16),
            jax.ShapeDtypeStruct((tm, patches, auxw), BF16),
        ),
        in_specs=[VMEM] * 4 + [ANY],
        out_specs=(ANY, ANY, ANY),
        scratch_shapes=[
            pltpu.VMEM((tm, patches, chunk), BF16),
            pltpu.VMEM((patches, auxw), BF16),
            DMA((3,)), DMA((tm,)), DMA((tm,)),
            DMA((3, tm)), DMA((tm,)), DMA((3, tm)), DMA((tm,)),
        ],
        compiler_params=talking(0),
        name="spatial_forward",
        cost_estimate=pl.CostEstimate(
            flops=6 * patches * patches * inner, bytes_accessed=4 * patches * inner,
            transcendentals=patches * patches * nheads,
        ),
    )(x, bc, raw, decay_rate, grad_out[0])

    rows = 64 if patches % 64 == 0 else 32
    block = lambda width: pl.BlockSpec((tm, rows, width), lambda i: (0, i, 0))
    whole = pl.BlockSpec((chunk, model), lambda i: (0, 0))
    base = (lax.axis_index("tm") * mine).astype(jnp.int32).reshape(1)
    grad_here, partial_out, partial_aux, grad_w = pl.pallas_call(
        functools.partial(temporal_kernel, nheads, mine, 16),
        grid=(patches // rows,),
        out_shape=(
            jax.ShapeDtypeStruct((tm, patches, chunk), BF16),
            jax.ShapeDtypeStruct((tm, patches, model), BF16),
            jax.ShapeDtypeStruct((tm, patches, auxw), BF16),
            jax.ShapeDtypeStruct((chunk, model), F32),
        ),
        in_specs=[SMEM, SMEM, SMEM, block(chunk), block(model), block(auxw), whole],
        out_specs=(block(chunk), block(model), block(auxw), whole),
        scratch_shapes=[pltpu.VMEM((tm, rows, chunk), BF16)],
        compiler_params=PARAMS,
        name="temporal",
        cost_estimate=pl.CostEstimate(
            flops=6 * tm * patches * chunk * model, bytes_accessed=8 * tm * patches * model,
            transcendentals=tm * patches * 128 * mine,
        ),
    )(base, decay_rate, skip_gain, spatial_here, go_all, aux_all, w_out)

    chips = tm // 2
    slots = lambda width: pltpu.VMEM((chips, patches, width), BF16)
    grad_x, grad_bc, grad_step, mixed_out = pl.pallas_call(
        functools.partial(backward_kernel, nheads, chunk, tm),
        out_shape=(
            jax.ShapeDtypeStruct((patches, inner), BF16),
            jax.ShapeDtypeStruct((patches, 2 * n2), BF16),
            jax.ShapeDtypeStruct((patches, 2 * nheads), BF16),
            jax.ShapeDtypeStruct((patches, model), BF16),
        ),
        in_specs=[VMEM] * 4 + [ANY] * 3,
        out_specs=(VMEM,) * 4,
        scratch_shapes=[pltpu.VMEM((tm, patches, chunk), BF16)]
        + [slots(model), slots(auxw)] * 3
        + [pltpu.VMEM((2, chips, patches, w), BF16) for w in (model, auxw)]
        + [DMA((3, chips)), DMA((tm,)), DMA((tm,))]
        + [DMA((2, chips))] * 3
        + [DMA((2, 2, chips))],
        compiler_params=talking(1),
        name="spatial_backward",
        cost_estimate=pl.CostEstimate(
            flops=12 * patches * patches * inner, bytes_accessed=6 * patches * inner,
            transcendentals=patches * patches * nheads,
        ),
    )(x, bc, raw, decay_rate, grad_here, partial_out, partial_aux)
    return (mixed_out[None], grad_x[None], grad_bc[None], grad_step[None], grad_w)


def solution(mesh):
    in_specs = (
        P(("clip", "tm"), None, None),
        P(("clip", "tm"), None, None),
        P(("clip", "tm"), None, None),
        P(),
        P(),
        P("tm", None),
        P(("clip", "tm"), None, None),
    )
    out_specs = (
        P(("clip", "tm"), None, None),
        P(("clip", "tm"), None, None),
        P(("clip", "tm"), None, None),
        P(("clip", "tm"), None, None),
        P(("clip", "tm"), None),
    )
    return jax.shard_map(
        functools.partial(on_device, tm=mesh.shape["tm"]),
        mesh=mesh, in_specs=in_specs, out_specs=out_specs, check_vma=False,
    )
```

```python
import functools

import jax
import jax.numpy as jnp
from jax import lax
from jax.experimental import pallas as pl
from jax.experimental.pallas import tpu as pltpu
from jax.sharding import PartitionSpec as P

F32 = jnp.float32
BF16 = jnp.bfloat16
HIGH = lax.Precision.HIGHEST
LANES = 128


def iota(shape, dim):
    return lax.broadcasted_iota(jnp.int32, shape, dim)


def mm(a, b, ca=1, cb=0, precision=None):
    return lax.dot_general(
        a, b, (((ca,), (cb,)), ((), ())), precision=precision, preferred_element_type=F32
    )


def softplus(raw):
    return jnp.maximum(raw, 0.0) + jnp.log(1.0 + jnp.exp(-jnp.abs(raw)))


DMA = pltpu.SemaphoreType.DMA


def picker(rows, base, count):
    r, c = iota((rows, LANES), 0), iota((rows, LANES), 1)
    return jnp.where((r == c + base) & (c < count), 1.0, 0.0).astype(BF16)


def decay_lanes(decay_ref):
    row = decay_ref[0:1, :]
    return jnp.concatenate([row, jnp.zeros((1, LANES - row.shape[1]), F32)], axis=1)


def steps_of(raw_bf, pick, decay_row, mask):
    raw = mm(raw_bf, pick)
    step = softplus(raw)
    cum = mm(mask, -step * decay_row, precision=HIGH)
    return raw, step, cum, step.T, cum.T


def weights_of(head, cum, cum_t, step_t):
    gap = cum[:, head : head + 1] - cum_t[head : head + 1, :]
    return jnp.exp(jnp.minimum(gap, 0.0)) * step_t[head : head + 1, :]


def step_grad(row_sums, col_sums_t, raw, step, decay_row, mask):
    col_sums = col_sums_t.T
    later = mm(mask, row_sums - col_sums, 0, 0, precision=HIGH)
    grad = col_sums / step - decay_row * later
    return grad / (1.0 + jnp.exp(-raw))


def remote(src, dst, send, recv, peer):
    return pltpu.make_async_remote_copy(
        src_ref=src, dst_ref=dst, send_sem=send, recv_sem=recv,
        device_id={"tm": peer}, device_id_type=pl.DeviceIdType.MESH,
    )


def greet_all(me, tm):
    barrier = pltpu.get_barrier_semaphore()
    for d in range(1, tm):
        pl.semaphore_signal(
            barrier, inc=1, device_id={"tm": lax.rem(me + d, tm)},
            device_id_type=pl.DeviceIdType.MESH,
        )
    pl.semaphore_wait(barrier, tm - 1)


def forward_kernel(
    nheads, chunk, tm,
    x_ref, bc_ref, raw_ref, decay_ref, go_ref,
    here_ref, go_all, aux_all,
    out_ref, aux_vm, own_sem, sp_send, sp_recv, go_send, go_recv, aux_send, aux_recv,
):
    length = x_ref.shape[0]
    n = bc_ref.shape[1] // 4
    me = lax.axis_index("tm")
    core = lax.rem(me, 2)
    partner = me + 1 - 2 * core
    chips, chip = tm // 2, lax.div(me, 2)
    aux_vm[:, : 2 * n] = bc_ref[:, 2 * n :]
    aux_vm[:, 2 * n :] = raw_ref[:, nheads:]
    own = [
        pltpu.make_async_copy(go_ref, go_all.at[me], own_sem.at[0]),
        pltpu.make_async_copy(aux_vm, aux_all.at[me], own_sem.at[1]),
    ]
    for copy in own:
        copy.start()
    greet_all(me, tm)
    gathers = ((aux_vm, aux_all, aux_send, aux_recv), (go_ref, go_all, go_send, go_recv))

    def hand_on(src, dst, send, recv, owner, right, left):
        @pl.when(right)
        def _():
            remote(src, dst.at[owner], send.at[0, owner], recv.at[owner], me + 2).start()

        @pl.when(left)
        def _():
            remote(src, dst.at[owner], send.at[1, owner], recv.at[owner], me - 2).start()

        remote(src, dst.at[owner], send.at[2, owner], recv.at[owner], partner).start()

    for src, dst, send, recv in gathers:
        hand_on(src, dst, send, recv, me, chip < chips - 1, chip > 0)

    mask = jnp.where(iota((length, length), 0) >= iota((length, length), 1), 1.0, 0.0)
    pick = picker(raw_ref.shape[1], 0, nheads)
    _, _, cum, step_t, cum_t = steps_of(raw_ref[...], pick, decay_lanes(decay_ref), mask)
    gram = mm(bc_ref[:, n : 2 * n], bc_ref[:, :n], 1, 1) * mask
    first = iota((length, LANES), 1) < LANES // 2
    for pair in range(nheads // 2):
        xp = x_ref[:, pair * LANES : (pair + 1) * LANES]
        ys = []
        for e in range(2):
            m = gram * weights_of(2 * pair + e, cum, cum_t, step_t)
            ys.append(mm(m.astype(BF16), xp))
        at = pair * LANES
        out_ref[at // chunk, :, at % chunk : at % chunk + LANES] = jnp.where(
            first, ys[0], ys[1]
        ).astype(BF16)

    sends = []
    own.append(pltpu.make_async_copy(out_ref.at[me], here_ref.at[me], own_sem.at[2]))
    own[-1].start()
    for d in range(1, tm):
        peer = lax.rem(me + d, tm)
        sends.append(
            remote(out_ref.at[peer], here_ref.at[me], sp_send.at[d], sp_recv.at[me], peer)
        )
        sends[-1].start()
    def passing(step, wait):
        for sign in (-1, 1):
            got = me + 2 * sign * step
            here = (chip >= step) if sign < 0 else (chip < chips - step)
            right = (chip < chips - 1) if sign < 0 else (chip < 0)
            left = (chip < 0) if sign < 0 else (chip > 0)

            @pl.when(here)
            def _():
                for src, dst, send, recv in gathers:
                    wait(src, dst, send, recv, got, right, left)

    def take(src, dst, send, recv, got, right, left):
        remote(src, dst.at[got], send.at[2, got], recv.at[got], partner).wait_recv()
        hand_on(dst.at[got], dst, send, recv, got, right, left)

    def sent(src, dst, send, recv, got, right, left):
        @pl.when(right)
        def _():
            remote(src, dst.at[got], send.at[0, got], recv.at[got], me + 2).wait_send()

        @pl.when(left)
        def _():
            remote(src, dst.at[got], send.at[1, got], recv.at[got], me - 2).wait_send()

        remote(src, dst.at[got], send.at[2, got], recv.at[got], partner).wait_send()

    for step in range(1, chips):
        passing(step, take)
    for src, dst, send, recv in gathers:
        for d in range(chips):
            got = lax.rem(partner + 2 * d, tm)
            remote(src, dst.at[got], send.at[2, got], recv.at[got], partner).wait_recv()
    for d in range(1, tm):
        got = lax.rem(me + d, tm)
        remote(out_ref.at[got], here_ref.at[got], sp_send.at[d], sp_recv.at[got], got).wait_recv()
    for copy in own:
        copy.wait()
    for copy in sends:
        copy.wait_send()
    for src, dst, send, recv in gathers:
        sent(src, dst, send, recv, me, chip < chips - 1, chip > 0)
    for step in range(1, chips):
        passing(step, sent)


def backward_kernel(
    nheads, chunk, tm,
    x_ref, bc_ref, raw_ref, decay_ref, grad_ref, part_ref, paux_ref,
    dx_ref, dbc_ref, draw_ref, out_ref,
    dy_ref, own_part, own_aux, in_part, in_aux, sum_part, sum_aux, far_part, far_aux,
    own_sem, dy_send, dy_recv, near_send, near_recv, far_send, far_recv,
):
    chips = tm // 2
    me = lax.axis_index("tm")
    core = lax.rem(me, 2)
    chip = lax.div(me, 2)
    partner = me + 1 - 2 * core
    own = [pltpu.make_async_copy(grad_ref.at[me], dy_ref.at[me], own_sem.at[0, 0])]
    kinds = (
        (part_ref, own_part, in_part, sum_part, far_part),
        (paux_ref, own_aux, in_aux, sum_aux, far_aux),
    )
    for k, (src, mine, _, _, _) in enumerate(kinds):
        for q in range(chips):
            own.append(pltpu.make_async_copy(src.at[2 * q + core], mine.at[q], own_sem.at[k + 1, q]))
    for copy in own:
        copy.start()
    greet_all(me, tm)
    sends, nears = [], []
    for k, (src, _, near, _, _) in enumerate(kinds):
        for q in range(chips):
            nears.append(
                remote(
                    src.at[2 * q + 1 - core], near.at[q], near_send.at[k, q], near_recv.at[k, q],
                    partner,
                )
            )
            nears[-1].start()
    for d in range(1, tm):
        peer = lax.rem(me + d, tm)
        sends.append(
            remote(grad_ref.at[peer], dy_ref.at[me], dy_send.at[d], dy_recv.at[me], peer)
        )
        sends[-1].start()
    for copy in own + nears:
        copy.wait()

    def hop(k, q, side):
        total, far = kinds[k][3], kinds[k][4]
        return remote(
            total.at[q], far.at[side, q], far_send.at[k, q], far_recv.at[k, side, q],
            lax.rem(me + tm + 2 - 4 * side, tm),
        )

    def forward(q, side):
        for k, (_, mine, near, total, far) in reversed(list(enumerate(kinds))):
            total[q] = (mine[q].astype(F32) + near[q].astype(F32)).astype(BF16)

            @pl.when((chip > 0) if side == 0 else (chip < chips - 1))
            def _():
                hop(k, q, side).wait_recv()
                total[q] = (
                    mine[q].astype(F32) + near[q].astype(F32) + far[side, q].astype(F32)
                ).astype(BF16)

            hop(k, q, side).start()

    def round_of(step):
        @pl.when(chips - 1 - step > chip)
        def _():
            forward(chips - 1 - step, 0)

        @pl.when(step < chip)
        def _():
            forward(step, 1)

    inner_chip = (chip > 0) & (chip < chips - 1)
    round_of(0)

    @pl.when(jnp.logical_not(inner_chip))
    def _():
        for step in range(1, chips - 1):
            round_of(step)

    length = x_ref.shape[0]
    n = bc_ref.shape[1] // 4
    mask = jnp.where(iota((length, length), 0) >= iota((length, length), 1), 1.0, 0.0)
    pick = picker(raw_ref.shape[1], 0, nheads)
    decay_row = decay_lanes(decay_ref)
    raw, step, cum, step_t, cum_t = steps_of(raw_ref[...], pick, decay_row, mask)
    b, c = bc_ref[:, :n], bc_ref[:, n : 2 * n]
    gram = mm(c, b, 1, 1) * mask
    lane = iota((length, LANES), 1)
    first = lane < LANES // 2
    sub = iota((LANES, length), 0)
    for d in range(1, tm):
        got = lax.rem(me + d, tm)
        remote(grad_ref.at[got], dy_ref.at[got], dy_send.at[d], dy_recv.at[got], got).wait_recv()

    dgram = jnp.zeros((length, length), F32)
    row_sums = jnp.zeros((length, LANES), F32)
    col_sums = jnp.zeros((LANES, length), F32)
    for pair in range(nheads // 2):
        if pair and pair % (nheads // 2 // (chips - 1) + 1) == 0:
            rnd = pair // (nheads // 2 // (chips - 1) + 1)

            @pl.when(inner_chip)
            def _():
                round_of(rnd)

        at = pair * LANES
        xp = x_ref[:, at : at + LANES]
        gp = dy_ref[at // chunk, :, at % chunk : at % chunk + LANES]
        dxs = []
        for e in range(2):
            head = 2 * pair + e
            ls = weights_of(head, cum, cum_t, step_t)
            m = gram * ls
            ge = jnp.where(first if e == 0 else ~first, gp, jnp.zeros_like(gp))
            dm = mm(ge, xp, 1, 1)
            dgram = dgram + dm * ls
            w = dm * m
            row_sums = jnp.where(lane == head, jnp.sum(w, axis=1, keepdims=True), row_sums)
            col_sums = jnp.where(sub == head, jnp.sum(w, axis=0, keepdims=True), col_sums)
            dxs.append(mm(m.astype(BF16), gp, 0, 0))
        dx_ref[:, at : at + LANES] = jnp.where(first, dxs[0], dxs[1]).astype(BF16)
    draw = step_grad(row_sums, col_sums, raw, step, decay_row, mask)
    draw_ref[:, :nheads] = draw[:, :nheads].astype(BF16)
    dgb = (dgram * mask).astype(BF16)
    dbc_ref[:, :n] = mm(dgb, c, 0, 0).astype(BF16)
    dbc_ref[:, n : 2 * n] = mm(dgb, b).astype(BF16)

    for k, (_, mine, near, total, far) in reversed(list(enumerate(kinds))):
        total[chip] = (mine[chip].astype(F32) + near[chip].astype(F32)).astype(BF16)
        for side in range(2):
            @pl.when((chip > 0) if side == 0 else (chip < chips - 1))
            def _():
                hop(k, chip, side).wait_recv()
                total[chip] = (total[chip].astype(F32) + far[side, chip].astype(F32)).astype(BF16)

    out_ref[...] = sum_part[chip]
    other = sum_aux[chip]
    dbc_ref[:, 2 * n :] = other[:, : 2 * n]
    draw_ref[:, nheads:] = other[:, 2 * n :]
    for copy in sends:
        copy.wait_send()
    for k in range(2):
        for q in range(chips):
            @pl.when(chip != q)
            def _():
                hop(k, q, 0).wait_send()


def temporal_kernel(
    nheads, mine, group,
    base_ref, decay_ref, skip_ref, x_ref, go_ref, aux_ref, w_ref,
    dx_ref, part_ref, daux_ref, gw_ref, mixed_ref,
):
    frames, patches, width = x_ref.shape
    n = (aux_ref.shape[2] - nheads) // 2
    base = base_ref[0]
    rows = frames * group
    ri, ci = iota((rows, rows), 0), iota((rows, rows), 1)
    mask = jnp.where((ri % group == ci % group) & (ri >= ci), 1.0, 0.0)
    pick = picker(nheads, base, mine)
    lane = iota((rows, LANES), 1)
    sub = iota((LANES, rows), 0)
    first = lane < LANES // 2
    lane1 = iota((1, LANES), 1)
    decay_row = jnp.zeros((1, LANES), F32)
    for h in range(mine):
        decay_row = jnp.where(lane1 == h, decay_ref[1, base + h], decay_row)
    w = w_ref[...]
    go = go_ref[...].reshape(frames * patches, go_ref.shape[2])
    carried = mm(go, w, 1, 1).astype(BF16).reshape(frames, patches, width)
    raws = mm(aux_ref[:, :, 2 * n :].reshape(frames * patches, nheads), pick)
    steps = softplus(raws)
    logs = (-steps * decay_row).reshape(frames, patches, LANES)
    raws, steps = (v.reshape(frames, patches, LANES) for v in (raws, steps))
    cums = [logs[0]]
    for f in range(1, frames):
        cums.append(cums[-1] + logs[f])
    cums = jnp.stack(cums)
    for part in range(patches // group):
        sl = slice(part * group, (part + 1) * group)
        x = x_ref[:, sl, :].reshape(rows, width)
        g = carried[:, sl, :].reshape(rows, width)
        aux = aux_ref[:, sl, :].reshape(rows, aux_ref.shape[2])
        b, c = aux[:, :n], aux[:, n : 2 * n]
        raw, step, cum = (v[:, sl, :].reshape(rows, LANES) for v in (raws, steps, cums))
        step_t, cum_t = step.T, cum.T
        gram = mm(c, b, 1, 1) * mask
        dgram = jnp.zeros((rows, rows), F32)
        row_sums = jnp.zeros((rows, LANES), F32)
        col_sums = jnp.zeros((LANES, rows), F32)
        for pair in range(mine // 2):
            at = pair * LANES
            xp, gp = x[:, at : at + LANES], g[:, at : at + LANES]
            ys, dxs = [], []
            for e in range(2):
                head = 2 * pair + e
                ls = weights_of(head, cum, cum_t, step_t)
                m = gram * ls
                mb = m.astype(BF16)
                ge = jnp.where(first if e == 0 else ~first, gp, jnp.zeros_like(gp))
                dm = mm(ge, xp, 1, 1)
                dgram = dgram + dm * ls
                wm = dm * m
                row_sums = jnp.where(lane == head, jnp.sum(wm, axis=1, keepdims=True), row_sums)
                col_sums = jnp.where(sub == head, jnp.sum(wm, axis=0, keepdims=True), col_sums)
                ys.append(mm(mb, xp))
                dxs.append(mm(mb, gp, 0, 0))
            skip = jnp.where(
                lane1 < LANES // 2, skip_ref[base + 2 * pair], skip_ref[base + 2 * pair + 1]
            )
            y = jnp.where(first, ys[0], ys[1]) + skip * xp.astype(F32)
            dx = jnp.where(first, dxs[0], dxs[1]) + skip * gp.astype(F32)
            mixed_ref[:, sl, at : at + LANES] = y.astype(BF16).reshape(frames, group, LANES)
            dx_ref[:, sl, at : at + LANES] = dx.astype(BF16).reshape(frames, group, LANES)
        col_sums = col_sums.T
        ends = (row_sums - col_sums).reshape(frames, group, LANES)
        later = [ends[frames - 1]]
        for f in range(frames - 2, -1, -1):
            later.append(later[-1] + ends[f])
        later = jnp.stack(later[::-1]).reshape(rows, LANES)
        draw = (col_sums / step - decay_row * later) / (1.0 + jnp.exp(-raw))
        placed = mm(draw.astype(BF16), pick, 1, 1)
        dgb = (dgram * mask).astype(BF16)
        shape = lambda v: v.astype(BF16).reshape(frames, group, v.shape[1])
        daux_ref[:, sl, :n] = shape(mm(dgb, c, 0, 0))
        daux_ref[:, sl, n : 2 * n] = shape(mm(dgb, b))
        daux_ref[:, sl, 2 * n :] = shape(placed)
    mixed = mixed_ref[...].reshape(frames * patches, width)
    part_ref[...] = mm(mixed, w).astype(BF16).reshape(part_ref.shape)

    @pl.when(pl.program_id(0) == 0)
    def _():
        gw_ref[...] = jnp.zeros_like(gw_ref)

    gw_ref[...] += mm(mixed, go, 0, 0)


VMEM = pl.BlockSpec(memory_space=pltpu.VMEM)
ANY = pl.BlockSpec(memory_space=pl.ANY)
SMEM = pl.BlockSpec(memory_space=pltpu.SMEM)
LIMIT = 60 * 1024 * 1024
PARAMS = pltpu.CompilerParams(vmem_limit_bytes=LIMIT)


def talking(number, limit=LIMIT):
    return pltpu.CompilerParams(
        vmem_limit_bytes=limit, collective_id=number, has_side_effects=True
    )


def on_device(x_inner, bc_inputs, step_raw, decay_rate, skip_gain, w_out, grad_out, tm):
    nheads = skip_gain.shape[0]
    _, patches, inner = x_inner.shape
    n2 = bc_inputs.shape[2] // 2
    model = w_out.shape[1]
    chunk = inner // tm
    mine = nheads // tm
    x, bc, raw = x_inner[0], bc_inputs[0], step_raw[0]
    auxw = n2 + nheads

    spatial_here, go_all, aux_all = pl.pallas_call(
        functools.partial(forward_kernel, nheads, chunk, tm),
        out_shape=(
            jax.ShapeDtypeStruct((tm, patches, chunk), BF16),
            jax.ShapeDtypeStruct((tm, patches, model), BF16),
            jax.ShapeDtypeStruct((tm, patches, auxw), BF16),
        ),
        in_specs=[VMEM] * 4 + [ANY],
        out_specs=(ANY, ANY, ANY),
        scratch_shapes=[
            pltpu.VMEM((tm, patches, chunk), BF16),
            pltpu.VMEM((patches, auxw), BF16),
            DMA((3,)), DMA((tm,)), DMA((tm,)),
            DMA((3, tm)), DMA((tm,)), DMA((3, tm)), DMA((tm,)),
        ],
        compiler_params=talking(0),
        name="spatial_forward",
        cost_estimate=pl.CostEstimate(
            flops=6 * patches * patches * inner, bytes_accessed=4 * patches * inner,
            transcendentals=patches * patches * nheads,
        ),
    )(x, bc, raw, decay_rate, grad_out[0])

    rows = 64 if patches % 64 == 0 else 32
    block = lambda width: pl.BlockSpec((tm, rows, width), lambda i: (0, i, 0))
    whole = pl.BlockSpec((chunk, model), lambda i: (0, 0))
    base = (lax.axis_index("tm") * mine).astype(jnp.int32).reshape(1)
    grad_here, partial_out, partial_aux, grad_w = pl.pallas_call(
        functools.partial(temporal_kernel, nheads, mine, 16),
        grid=(patches // rows,),
        out_shape=(
            jax.ShapeDtypeStruct((tm, patches, chunk), BF16),
            jax.ShapeDtypeStruct((tm, patches, model), BF16),
            jax.ShapeDtypeStruct((tm, patches, auxw), BF16),
            jax.ShapeDtypeStruct((chunk, model), F32),
        ),
        in_specs=[SMEM, SMEM, SMEM, block(chunk), block(model), block(auxw), whole],
        out_specs=(block(chunk), block(model), block(auxw), whole),
        scratch_shapes=[pltpu.VMEM((tm, rows, chunk), BF16)],
        compiler_params=PARAMS,
        name="temporal",
        cost_estimate=pl.CostEstimate(
            flops=6 * tm * patches * chunk * model, bytes_accessed=8 * tm * patches * model,
            transcendentals=tm * patches * 128 * mine,
        ),
    )(base, decay_rate, skip_gain, spatial_here, go_all, aux_all, w_out)

    chips = tm // 2
    slots = lambda width: pltpu.VMEM((chips, patches, width), BF16)
    grad_x, grad_bc, grad_step, mixed_out = pl.pallas_call(
        functools.partial(backward_kernel, nheads, chunk, tm),
        out_shape=(
            jax.ShapeDtypeStruct((patches, inner), BF16),
            jax.ShapeDtypeStruct((patches, 2 * n2), BF16),
            jax.ShapeDtypeStruct((patches, 2 * nheads), BF16),
            jax.ShapeDtypeStruct((patches, model), BF16),
        ),
        in_specs=[VMEM] * 4 + [ANY] * 3,
        out_specs=(VMEM,) * 4,
        scratch_shapes=[pltpu.VMEM((tm, patches, chunk), BF16)]
        + [slots(model), slots(auxw)] * 3
        + [pltpu.VMEM((2, chips, patches, w), BF16) for w in (model, auxw)]
        + [DMA((3, chips)), DMA((tm,)), DMA((tm,))]
        + [DMA((2, chips))] * 3
        + [DMA((2, 2, chips))],
        compiler_params=talking(1, 40 * 1024 * 1024),
        name="spatial_backward",
        cost_estimate=pl.CostEstimate(
            flops=12 * patches * patches * inner, bytes_accessed=6 * patches * inner,
            transcendentals=patches * patches * nheads,
        ),
    )(x, bc, raw, decay_rate, grad_here, partial_out, partial_aux)
    return (mixed_out[None], grad_x[None], grad_bc[None], grad_step[None], grad_w)


def solution(mesh):
    in_specs = (
        P(("clip", "tm"), None, None),
        P(("clip", "tm"), None, None),
        P(("clip", "tm"), None, None),
        P(),
        P(),
        P("tm", None),
        P(("clip", "tm"), None, None),
    )
    out_specs = (
        P(("clip", "tm"), None, None),
        P(("clip", "tm"), None, None),
        P(("clip", "tm"), None, None),
        P(("clip", "tm"), None, None),
        P(("clip", "tm"), None),
    )
    return jax.shard_map(
        functools.partial(on_device, tm=mesh.shape["tm"]),
        mesh=mesh, in_specs=in_specs, out_specs=out_specs, check_vma=False,
    )
```
